32 devices in a mesh: enc: 4 (over z), bin: 4 (over x, core), off: 2 (over y).
Axes of the slice: x: 2, y: 2, z: 4, core: 2. Of those that a mesh axis runs over, the one named last changes fastest.
Arguments:
- encoder_in: bfloat16 [512, 1536], P(('bin', 'off'), 'enc'), may hold values from -6 to 6
- gain_enc: float32 [512], P(('bin', 'off')), may hold values from 0.1 to 1.9
- conv_one: bfloat16 [3, 512, 512], P(None, ('bin', 'off')), may hold values from -0.15625 to 0.15625
- proj_weight: bfloat16 [2, 512, 32], P(None, ('bin', 'off')), may hold values from -0.25 to 0.25
- conv_two: bfloat16 [9, 32, 32], replicated, may hold values from -0.375 to 0.375
- head_weight: float32 [32], replicated, may hold values from -1 to 1
- target: bfloat16 [1536, 1024], P('bin', ('enc', 'off')), may hold values from -8 to 8
- valid_bins: int32 [1536], replicated, may hold values 0 or 1
- offset_limit: int32 [1536], replicated, may hold values from 512 to 1024
- dilations: int32 [2], replicated, may hold values from 1 to 8, as said below
Outputs:
- prediction: float32 [1536, 1024], P('bin', ('enc', 'off'))
- loss_mean: float32 [1], replicated
- grad_conv_two: float32 [9, 32, 32], replicated
- grad_proj: float32 [2, 512, 32], P(None, ('bin', 'off'))
- grad_conv_one: float32 [3, 512, 512], P(None, ('bin', 'off'), 'enc')
The draws below stay inside these ranges and needn't reach their ends.
Inputs may be any that keep to these rules, and one draw needn't show every extreme that they name: dilations[0] is the dilation of the 1-D layer and dilations[1] that of the 2-D layer; one of the two equals 8, the other is smaller.
All inputs are finite; a program needn't handle non-finite values.
Results may differ from the reference program's by a relative error of at most 0.0013.
The reference program's roundings to bfloat16 on the way (of `activ`, `hidden`, `embed`, `band_act`, `dres`, `grad_embed` and `dhidden`) count: a program that leaves them out, or rounds other values in their place, can miss the bound.
Values may be sent and summed in bfloat16 or wider, within the bound.
A program may use at most 192 MiB of HBM per device.

```python
import jax
import jax.numpy as jnp
from jax import lax

C1 = 512
C2 = 32
BAND_TILE_BINS = 384
KD = 128
LARGEST_DILATION = 8
L = 1536
K = 1024
N_ENC = 4
N_BIN = 4
N_OFF = 2


def draw_dilations(key, part):
    first, second = jax.random.split(jax.random.fold_in(key, 11))
    other = jax.random.randint(first, (), 1, LARGEST_DILATION).astype(jnp.int32)
    order = jax.random.randint(second, (), 0, 2)
    largest = jnp.full((), LARGEST_DILATION, jnp.int32)
    return jnp.where(order == 1, jnp.stack([largest, other]), jnp.stack([other, largest])).astype(jnp.int32)


def draw_target(key, part):
    offsets = jnp.arange(K, dtype=jnp.float32) / K
    scale = 0.5 + 1.5 * offsets
    values = jax.random.normal(jax.random.fold_in(key, 23), (L, K), jnp.float32) * scale[None, :]
    return jnp.clip(values, -8.0, 8.0).astype(jnp.bfloat16)


def plant(entries, key, low, high):
    longest = entries.shape.index(max(entries.shape))
    spots = []
    for shift in (0, 1):
        where = [jax.random.randint(jax.random.fold_in(key, axis), (), 0, length) for axis, length in enumerate(entries.shape)]
        where[longest] = (where[longest] + shift) % entries.shape[longest]
        spots.append(tuple(where))
    return entries.at[spots[0]].set(low).at[spots[1]].set(high)


def shard_levels(key, dims, pieces, low, top_value):
    def one(position, parts):
        steps = jax.random.uniform(jax.random.fold_in(jax.random.fold_in(key, 6), position), (parts,), jnp.float32, low / len(pieces), top_value / len(pieces))
        return jnp.repeat(jnp.exp(steps), dims[position] // parts).reshape((-1,) + (1,) * (len(dims) - position - 1))

    gain = one(*pieces[0])
    for cut in pieces[1:]:
        gain = gain * one(*cut)
    return gain


def scatter_about(stream_key, extent, spread, reach, cuts=(), kind=jnp.bfloat16):
    array = spread * jax.random.normal(stream_key, extent, jnp.float32)
    if cuts:
        array = array * shard_levels(stream_key, extent, cuts, -0.22, 0.18)
    return jnp.clip(array, -reach, reach).astype(kind)


def setup_inputs(seed: int = 0) -> dict:
    splits = jax.random.split(jax.random.key(seed), 11)
    encoder_in = scatter_about(splits[0], (C1, L), 1.0, 6.0, ((0, 8), (1, 4)))
    gain_enc = jnp.clip(1.0 + 0.18 * jax.random.normal(splits[1], (C1,), jnp.float32), 0.1, 1.9)
    conv_one = scatter_about(splits[2], (3, C1, C1), (3 * C1) ** -0.5, 0.15625, ((1, 8),))
    proj_weight = scatter_about(splits[3], (2, C1, C2), C1 ** -0.5, 0.25, ((1, 8),))
    conv_two = scatter_about(splits[4], (9, C2, C2), (9 * C2) ** -0.5, 0.375)
    head_weight = scatter_about(splits[5], (C2,), C2 ** -0.5, 1.0, (), jnp.float32)
    target = draw_target(jax.random.fold_in(splits[10], 71), 0)
    valid_bins = plant((jax.random.randint(splits[7], (L,), 0, 8) < 7).astype(jnp.int32), jax.random.fold_in(splits[7], 1), 0, 1)
    offset_limit = plant(jax.random.randint(splits[8], (L,), K // 2, K + 1), jax.random.fold_in(splits[8], 1), K // 2, K).astype(jnp.int32)
    dilations = draw_dilations(jax.random.fold_in(splits[10], 71), 0)
    return {"encoder_in": encoder_in, "gain_enc": gain_enc, "conv_one": conv_one, "proj_weight": proj_weight, "conv_two": conv_two, "head_weight": head_weight, "target": target, "valid_bins": valid_bins, "offset_limit": offset_limit, "dilations": dilations}


def rounded(values):
    return lax.optimization_barrier(values.astype(jnp.bfloat16)).astype(jnp.float32)


def indices(*values):
    return tuple(jnp.asarray(value).astype(jnp.int32) for value in values)


def hankel(window, tile_rows, tile_cols):
    chans = window.shape[0]
    width = tile_rows + tile_cols
    base = window[:, :width - 1]
    tiled = jnp.broadcast_to(base[:, None, :], (chans, tile_rows, width - 1)).reshape(chans, tile_rows * (width - 1))
    tiled = jnp.pad(tiled, ((0, 0), (0, tile_rows)))
    return tiled.reshape(chans, tile_rows, width)[:, :, :tile_cols]


def diagonal_sums(tile):
    chans, tile_rows, tile_cols = tile.shape
    width = tile_rows + tile_cols
    padded_input = jnp.pad(tile, ((0, 0), (0, 0), (0, tile_rows)))
    flat = padded_input.reshape(chans, tile_rows * width)[:, :tile_rows * (width - 1)]
    return jnp.sum(flat.reshape(chans, tile_rows, width - 1), axis=1)


def count_cells(valid_bins, offset_limit):
    sequence_length = valid_bins.shape[0]
    running = jnp.concatenate([jnp.zeros((1,), jnp.int32), jnp.cumsum(valid_bins).astype(jnp.int32)])
    places = jnp.arange(sequence_length, dtype=jnp.int32)
    farthest = jnp.minimum(places + offset_limit.astype(jnp.int32), sequence_length)
    inside = jnp.take(running, farthest) - jnp.take(running, places)
    return jnp.sum(valid_bins.astype(jnp.int32) * inside).astype(jnp.float32)


def reference(encoder_in, gain_enc, conv_one, proj_weight, conv_two, head_weight, target, valid_bins, offset_limit, dilations):
    highest = lax.Precision.HIGHEST
    first_dilation = dilations[0].astype(jnp.int32)
    second_dilation = dilations[1].astype(jnp.int32)
    sequence_length = BAND_TILE_BINS * N_BIN
    window_extent = KD * N_ENC * N_OFF
    second_channels = conv_two.shape[1]
    activ = rounded(jax.nn.gelu(gain_enc[:, None] * encoder_in.astype(jnp.float32)))
    padded_input = jnp.pad(activ, ((0, 0), (LARGEST_DILATION, LARGEST_DILATION)))
    section_list = [lax.dynamic_slice_in_dim(padded_input, indices(LARGEST_DILATION + (kernel_tap_index - 1) * first_dilation)[0], sequence_length, 1) for kernel_tap_index in range(3)]
    conv_out = jnp.zeros((conv_one.shape[1], sequence_length), jnp.float32)
    for kernel_tap_index in range(3):
        conv_out = conv_out + jnp.dot(conv_one[kernel_tap_index].astype(jnp.float32), section_list[kernel_tap_index], precision=highest)
    hidden = rounded(encoder_in.astype(jnp.float32) + conv_out)
    embed = rounded(jnp.einsum("kce,ci->kei", proj_weight.astype(jnp.float32), hidden, precision=highest))
    border_width = 2 * LARGEST_DILATION
    wide_rows = BAND_TILE_BINS + 4 * LARGEST_DILATION
    middle_rows = BAND_TILE_BINS + 2 * LARGEST_DILATION
    near_ext = jnp.pad(embed[0], ((0, 0), (border_width, border_width + BAND_TILE_BINS)))
    far_ext = jnp.pad(embed[1], ((0, 0), (border_width, window_extent + border_width + BAND_TILE_BINS)))
    mask_ext = jnp.pad(valid_bins.astype(jnp.float32), (LARGEST_DILATION, window_extent + LARGEST_DILATION + BAND_TILE_BINS))
    limit_ext = jnp.pad(offset_limit.astype(jnp.int32), (LARGEST_DILATION, LARGEST_DILATION + BAND_TILE_BINS))
    target_ext = jnp.pad(target.astype(jnp.float32), ((LARGEST_DILATION, LARGEST_DILATION + BAND_TILE_BINS), (0, 0)))
    denom = 1.0 + count_cells(valid_bins, offset_limit)
    weights_two = conv_two.astype(jnp.float32)
    shifts = [(bin_displacement, offset_displacement) for bin_displacement in (-1, 0, 1) for offset_displacement in (-1, 0, 1)]
    offs_ids = jnp.arange(window_extent, dtype=jnp.int32)

    def block(carry, block_index):
        buffer, grad_band, error_sum = carry
        start = (block_index * BAND_TILE_BINS).astype(jnp.int32)
        row_ids = start - border_width + jnp.arange(wide_rows, dtype=jnp.int32)
        inside = ((row_ids >= 0) & (row_ids < sequence_length)).astype(jnp.float32)
        near_rows = lax.dynamic_slice_in_dim(near_ext, start, wide_rows, 1)
        far_rows = hankel(lax.dynamic_slice_in_dim(far_ext, start, wide_rows + window_extent, 1), wide_rows, window_extent)
        pair_sum = near_rows[:, :, None] + far_rows
        band_act = rounded(jnp.maximum(pair_sum, 0.0) * inside[None, :, None])
        activation_padded = jnp.pad(band_act, ((0, 0), (0, 0), (LARGEST_DILATION, LARGEST_DILATION)))
        band_conv = jnp.zeros((second_channels, middle_rows, window_extent), jnp.float32)
        for kernel_tap_index, (bin_displacement, offset_displacement) in enumerate(shifts):
            section_index = lax.dynamic_slice(activation_padded, indices(0, LARGEST_DILATION + bin_displacement * second_dilation, LARGEST_DILATION + offset_displacement * second_dilation), (second_channels, middle_rows, window_extent))
            band_conv = band_conv + jnp.einsum("ef,exy->fxy", weights_two[kernel_tap_index], section_index, precision=highest)
        pair_mid = pair_sum[:, LARGEST_DILATION:LARGEST_DILATION + middle_rows]
        resid = pair_mid + band_conv
        pred_mid = jnp.sum(head_weight[:, None, None] * jnp.maximum(resid, 0.0), axis=0)
        mask_rows = lax.dynamic_slice_in_dim(mask_ext, start, middle_rows)
        mask_far = hankel(lax.dynamic_slice_in_dim(mask_ext, start, middle_rows + window_extent)[None, :], middle_rows, window_extent)[0]
        limit_rows = lax.dynamic_slice_in_dim(limit_ext, start, middle_rows)
        weight = mask_rows[:, None] * mask_far * (offs_ids[None, :] < limit_rows[:, None]).astype(jnp.float32)
        target_rows = lax.dynamic_slice_in_dim(target_ext, start, middle_rows, 0)
        differ = pred_mid - target_rows
        dpred = 2.0 * weight * differ / denom
        dres = rounded(head_weight[:, None, None] * dpred[None] * (resid > 0.0).astype(jnp.float32))
        own_weight = weight[LARGEST_DILATION:LARGEST_DILATION + BAND_TILE_BINS]
        own_differ = differ[LARGEST_DILATION:LARGEST_DILATION + BAND_TILE_BINS]
        error_sum = error_sum + jnp.sum(own_weight * own_differ * own_differ)
        dres_own = dres[:, LARGEST_DILATION:LARGEST_DILATION + BAND_TILE_BINS]
        residual_grad_padded = jnp.pad(dres, ((0, 0), (0, 0), (LARGEST_DILATION, LARGEST_DILATION)))
        dact = jnp.zeros((second_channels, BAND_TILE_BINS, window_extent), jnp.float32)
        for kernel_tap_index, (bin_displacement, offset_displacement) in enumerate(shifts):
            activation_section = lax.dynamic_slice(activation_padded, indices(0, border_width + bin_displacement * second_dilation, LARGEST_DILATION + offset_displacement * second_dilation), (second_channels, BAND_TILE_BINS, window_extent))
            grad_band = grad_band.at[kernel_tap_index].add(jnp.einsum("exy,fxy->ef", activation_section, dres_own, precision=highest))
            residual_grad_section = lax.dynamic_slice(residual_grad_padded, indices(0, LARGEST_DILATION - bin_displacement * second_dilation, LARGEST_DILATION - offset_displacement * second_dilation), (second_channels, BAND_TILE_BINS, window_extent))
            dact = dact + jnp.einsum("ef,fxy->exy", weights_two[kernel_tap_index], residual_grad_section, precision=highest)
        pair_own = pair_sum[:, border_width:border_width + BAND_TILE_BINS]
        dpair = dres_own + dact * (pair_own > 0.0).astype(jnp.float32)
        near_grad = jnp.sum(dpair, axis=2)
        far_grad = diagonal_sums(dpair)
        old_near = lax.dynamic_slice(buffer, indices(0, 0, start), (1, second_channels, BAND_TILE_BINS))
        buffer = lax.dynamic_update_slice(buffer, old_near + near_grad[None], indices(0, 0, start))
        old_far = lax.dynamic_slice(buffer, indices(1, 0, start), (1, second_channels, BAND_TILE_BINS + window_extent - 1))
        buffer = lax.dynamic_update_slice(buffer, old_far + far_grad[None], indices(1, 0, start))
        return (buffer, grad_band, error_sum), pred_mid[LARGEST_DILATION:LARGEST_DILATION + BAND_TILE_BINS]

    init = (jnp.zeros((2, second_channels, sequence_length + window_extent + BAND_TILE_BINS), jnp.float32), jnp.zeros((9, second_channels, second_channels), jnp.float32), jnp.zeros((), jnp.float32))
    (buffer, grad_band, error_sum), preds = lax.scan(block, init, jnp.arange(sequence_length // BAND_TILE_BINS, dtype=jnp.int32))
    prediction = preds.reshape(sequence_length, window_extent)
    grad_embed = rounded(buffer[:, :, :sequence_length])
    dhidden = rounded(jnp.einsum("kce,kei->ci", proj_weight.astype(jnp.float32), grad_embed, precision=highest))
    grad_proj = jnp.einsum("ci,kei->kce", hidden, grad_embed, precision=highest)
    grad_conv_one = jnp.stack([jnp.einsum("ji,ci->jc", dhidden, section_list[kernel_tap_index], precision=highest) for kernel_tap_index in range(3)])
    loss_mean = (error_sum / denom).reshape(1)
    return prediction, loss_mean, grad_band, grad_proj, grad_conv_one
```

```python
import functools

import jax
import jax.numpy as jnp
from jax import lax
from jax.experimental import pallas as pl
from jax.experimental.pallas import tpu as pltpu
from jax.sharding import PartitionSpec as P

LARGEST_DILATION = 8


def with_halo(cells, sides, width):
    for axis, dim in sides:
        count = lax.axis_size(axis)
        ends = count - 1
        head = lax.slice_in_dim(cells, 0, width, axis=dim)
        tail = lax.slice_in_dim(cells, cells.shape[dim] - width, cells.shape[dim], axis=dim)
        cells = jnp.concatenate(
            [
                lax.ppermute(tail, axis, [(i, (i + 1) % count) for i in range(ends)]),
                cells,
                lax.ppermute(head, axis, [((i + 1) % count, i) for i in range(ends)]),
            ],
            axis=dim,
        )
    return cells


def count_cells(valid_bins, offset_limit):
    sequence_length = valid_bins.shape[0]
    places = jnp.arange(sequence_length, dtype=jnp.int32)
    gap = places[None, :] - places[:, None]
    scored = (gap >= 0) & (gap < offset_limit[:, None])
    inside = jnp.sum(jnp.where(scored, valid_bins[None, :], 0), axis=1)
    return jnp.sum(valid_bins * inside).astype(jnp.float32)


def round_up(value, step):
    return (value + step - 1) // step * step


def band_body(
    edge,
    rows,
    unroll,
    dil_ref,
    place_ref,
    denom_ref,
    near_ref,
    far_ref,
    fmask_ref,
    lanes_ref,
    limit_ref,
    target_ref,
    head_ref,
    wfwd_ref,
    wback_ref,
    pred_ref,
    err_ref,
    gband_ref,
    gnear_ref,
    gfar_ref,
    far_rolled,
    mask_rolled,
    near_shift,
    stack,
    resid_acc,
    dact_acc,
    own_grad,
):
    chans, width = near_ref.shape
    wide = far_ref.shape[1]
    d = dil_ref[0]
    offs_first = place_ref[0]
    offs_count = place_ref[1]
    denom = denom_ref[0]
    all_rows = rows + 4 * edge
    last = rows + 3 * edge

    def loop(start, stop, body, init):
        def step(index, carry):
            for inner in range(unroll):
                carry = body(start + index * unroll + inner, carry)
            return carry

        return lax.fori_loop(0, (stop - start) // unroll, step, init)

    near_shift[1] = near_ref[...]
    near_shift[0] = pltpu.roll(near_ref[...], d, 1)
    near_shift[2] = pltpu.roll(near_ref[...], width - d, 1)

    def fill(k, carry):
        shift = lax.rem(wide - k, wide)
        far_rolled[k] = pltpu.roll(far_ref[...], shift, 1)[:, :width].astype(jnp.bfloat16)
        mask_rolled[k] = pltpu.roll(fmask_ref[...], shift, 1)[:, :width]
        return carry

    loop(0, all_rows + 2 * edge, fill, 0)

    def clear(r, carry):
        resid_acc[r + edge] = near_ref[...] + far_rolled[r + edge].astype(jnp.float32)
        dact_acc[r] = jnp.zeros((chans, width), jnp.float32)
        return carry

    loop(0, all_rows, clear, 0)
    for r in list(range(edge)) + list(range(last, all_rows)):
        own_grad[r] = jnp.zeros((chans, width), jnp.bfloat16)

    def forward(r, carry):
        offs = offs_first + r - 2 * edge
        inside = jnp.where((offs >= 0) & (offs < offs_count), 1.0, 0.0)
        for a in range(3):
            cells = near_shift[a] + far_rolled[r + edge + (a - 1) * d].astype(jnp.float32)
            cells = jnp.maximum(cells, 0.0) * inside
            stack[r, a * chans : (a + 1) * chans, :] = cells.astype(jnp.bfloat16)
        taps = jnp.dot(wfwd_ref[...], stack[r], preferred_element_type=jnp.float32)
        for b in range(3):
            spot = r + edge - (b - 1) * d
            resid_acc[spot] = resid_acc[spot] + taps[b * chans : (b + 1) * chans]
        return carry

    loop(0, all_rows, forward, 0)

    def middle(r, err):
        resid = resid_acc[r + edge]
        head = head_ref[...]
        pred = jnp.sum(head * jnp.maximum(resid, 0.0), axis=0, keepdims=True)
        pred_ref[pl.ds(r - edge, 1), :] = pred
        offs = offs_first + r - 2 * edge
        inside = jnp.where((offs >= 0) & (offs < offs_count), 1.0, 0.0)
        own_row = jnp.where((r >= 2 * edge) & (r < rows + 2 * edge), 1.0, 0.0)
        weight = (
            lanes_ref[0:1, :]
            * mask_rolled[r + edge][0:1, :]
            * jnp.where(offs < limit_ref[...], inside, 0.0)
        )
        differ = pred - target_ref[pl.ds(r - edge, 1), :]
        own = lanes_ref[1:2, :] * own_row
        err = err + weight * differ * differ * own
        dpred = 2.0 * weight * differ / denom
        dres = jnp.where(resid > 0.0, head * dpred, 0.0).astype(jnp.bfloat16).astype(jnp.float32)
        own_grad[r] = (dres * own).astype(jnp.bfloat16)
        shifted = jnp.concatenate(
            [
                pltpu.roll(dres, width - d, 1).astype(jnp.bfloat16),
                dres.astype(jnp.bfloat16),
                pltpu.roll(dres, d, 1).astype(jnp.bfloat16),
            ],
            axis=0,
        )
        taps = jnp.dot(wback_ref[...], shifted, preferred_element_type=jnp.float32)
        for b in range(3):
            spot = r + (b - 1) * d
            dact_acc[spot] = dact_acc[spot] + taps[b * chans : (b + 1) * chans]
        return err

    err = loop(edge, last, middle, jnp.zeros((1, width), jnp.float32))
    err_ref[...] = err

    def weigh(r, total):
        grads = jnp.concatenate([own_grad[r - (b - 1) * d] for b in range(3)], axis=0)
        return total + lax.dot_general(
            stack[r], grads, (((1,), (1,)), ((), ())), preferred_element_type=jnp.float32
        )

    gband_ref[...] = loop(edge, last, weigh, jnp.zeros((3 * chans, 3 * chans), jnp.float32))

    own_near = jnp.where(lanes_ref[1:2, :] > 0.0, near_ref[...], -jnp.inf)
    gnear_ref[...] = jnp.zeros(gnear_ref.shape, jnp.float32)
    gfar_ref[...] = jnp.zeros(gfar_ref.shape, jnp.float32)
    blank = jnp.zeros((chans, wide - width), jnp.float32)
    near_shift[0] = own_near

    def collect(r, carry):
        pair = near_shift[0] + far_rolled[r + edge].astype(jnp.float32)
        dpair = own_grad[r].astype(jnp.float32) + jnp.where(pair > 0.0, dact_acc[r], 0.0)
        gnear_ref[...] += dpair
        gfar_ref[...] += pltpu.roll(jnp.concatenate([dpair, blank], axis=1), r + edge, 1)
        return carry

    loop(2 * edge, rows + 2 * edge, collect, 0)


def band(near, far, fmask, lanes, limits, target, head, wfwd, wback, dil, place, denom, rows):
    chans, width = near.shape
    wide = far.shape[1]
    edge = LARGEST_DILATION
    all_rows = rows + 4 * edge
    smem = pl.BlockSpec(memory_space=pltpu.SMEM)
    vmem = pl.BlockSpec(memory_space=pltpu.VMEM)
    return pl.pallas_call(
        functools.partial(band_body, edge, rows, 4),
        out_shape=(
            jax.ShapeDtypeStruct((rows + 2 * edge, width), jnp.float32),
            jax.ShapeDtypeStruct((1, width), jnp.float32),
            jax.ShapeDtypeStruct((3 * chans, 3 * chans), jnp.float32),
            jax.ShapeDtypeStruct((chans, width), jnp.float32),
            jax.ShapeDtypeStruct((chans, wide), jnp.float32),
        ),
        in_specs=[smem] * 3 + [vmem] * 9,
        out_specs=(vmem,) * 5,
        scratch_shapes=[
            pltpu.VMEM((all_rows + 2 * edge, chans, width), jnp.bfloat16),
            pltpu.VMEM((all_rows + 2 * edge, 8, width), jnp.float32),
            pltpu.VMEM((3, chans, width), jnp.float32),
            pltpu.VMEM((all_rows, 3 * chans, width), jnp.bfloat16),
            pltpu.VMEM((all_rows + 2 * edge, chans, width), jnp.float32),
            pltpu.VMEM((all_rows, chans, width), jnp.float32),
            pltpu.VMEM((all_rows, chans, width), jnp.bfloat16),
        ],
        compiler_params=pltpu.CompilerParams(vmem_limit_bytes=60 * 1024 * 1024),
        cost_estimate=pl.CostEstimate(flops=4000000000, bytes_accessed=2000000, transcendentals=0),
        name="band",
    )(dil, place, denom, near, far, fmask, lanes, limits, target, head, wfwd, wback)


def shards(
    encoder_in,
    gain_enc,
    conv_one,
    proj_weight,
    conv_two,
    head_weight,
    target,
    valid_bins,
    offset_limit,
    dilations,
):
    chans, encoder_bins = encoder_in.shape
    width_in = conv_one.shape[2]
    second_channels = conv_two.shape[1]
    tile_rows, tile_cols = target.shape
    first_dilation = dilations[0]
    second_dilation = dilations[1]
    activ = jax.nn.gelu(gain_enc[:, None] * encoder_in.astype(jnp.float32)).astype(jnp.bfloat16)
    framed = with_halo(activ, (("enc", 1),), LARGEST_DILATION)
    channel_count = lax.all_gather(framed, ("bin", "off"), axis=0, tiled=True)
    stacked_enc = jnp.concatenate(
        [
            lax.dynamic_slice_in_dim(
                channel_count,
                LARGEST_DILATION + (kernel_tap_index - 1) * first_dilation,
                encoder_bins,
                1,
            )
            for kernel_tap_index in range(3)
        ],
        axis=0,
    )
    weight_one = jnp.transpose(conv_one, (1, 0, 2)).reshape(chans, 3 * width_in)
    conv_out = jnp.dot(weight_one, stacked_enc, preferred_element_type=jnp.float32)
    hidden = (encoder_in.astype(jnp.float32) + conv_out).astype(jnp.bfloat16)
    proj_rows = jnp.transpose(proj_weight, (0, 2, 1)).reshape(2 * second_channels, chans)
    partial_embed = jnp.dot(proj_rows, hidden, preferred_element_type=jnp.float32)
    summed = lax.psum(partial_embed, ("bin", "off")).astype(jnp.bfloat16)
    embed = lax.all_gather(summed, "enc", axis=1, tiled=True)
    sequence_length = embed.shape[1]
    window_extent = tile_cols * lax.axis_size("enc") * lax.axis_size("off")
    row_start = lax.axis_index("bin") * tile_rows
    offs_start = (lax.axis_index("enc") * lax.axis_size("off") + lax.axis_index("off")) * tile_cols
    edge = LARGEST_DILATION
    width = round_up(tile_rows + 4 * edge, 128)
    wide = round_up(tile_rows + tile_cols + 10 * edge, 128)
    bin_ids = row_start - 2 * edge + jnp.arange(width, dtype=jnp.int32)
    inside = (bin_ids >= 0) & (bin_ids < sequence_length)
    near = lax.dynamic_slice_in_dim(
        jnp.pad(embed[:second_channels].astype(jnp.float32), ((0, 0), (2 * edge, width))),
        row_start,
        width,
        1,
    )
    near = jnp.where(inside[None, :], near, -jnp.inf)
    far = lax.dynamic_slice_in_dim(
        jnp.pad(
            embed[second_channels:].astype(jnp.float32), ((0, 0), (5 * edge, window_extent + wide))
        ),
        row_start + offs_start,
        wide,
        1,
    )
    mask_float = valid_bins.astype(jnp.float32)
    far_mask = lax.dynamic_slice_in_dim(
        jnp.pad(mask_float, (5 * edge, window_extent + wide)), row_start + offs_start, wide
    )
    near_mask = lax.dynamic_slice_in_dim(
        jnp.pad(mask_float, (2 * edge, width)), row_start, width
    )
    limits = lax.dynamic_slice_in_dim(jnp.pad(offset_limit, (2 * edge, width)), row_start, width)
    spots = jnp.arange(width, dtype=jnp.int32)
    framed_lane = (spots >= edge) & (spots < tile_rows + 3 * edge)
    own_lane = (spots >= 2 * edge) & (spots < tile_rows + 2 * edge)
    lanes = jnp.stack([jnp.where(framed_lane, near_mask, 0.0), own_lane.astype(jnp.float32)])
    lanes = jnp.pad(lanes, ((0, 6), (0, 0)))
    denom = 1.0 + count_cells(valid_bins, offset_limit)
    framed_target = with_halo(target, (("bin", 0), (("enc", "off"), 1)), edge)
    target_rows = jnp.pad(
        framed_target.T.astype(jnp.float32), ((0, 0), (edge, width - tile_rows - 3 * edge))
    )
    taps = conv_two.reshape(3, 3, second_channels, second_channels)
    weight_fwd = jnp.transpose(taps, (1, 3, 0, 2)).reshape(3 * second_channels, 3 * second_channels)
    weight_back = jnp.transpose(taps, (1, 2, 0, 3)).reshape(3 * second_channels, 3 * second_channels)
    pred_rows, error_lanes, grad_taps, near_lanes, far_lanes = band(
        near,
        far,
        jnp.broadcast_to(far_mask[None, :], (8, wide)),
        lanes,
        limits[None, :],
        target_rows,
        jnp.broadcast_to(head_weight[:, None], (second_channels, width)),
        weight_fwd,
        weight_back,
        second_dilation.reshape(1),
        jnp.stack([offs_start, jnp.full((), window_extent, jnp.int32)]).astype(jnp.int32),
        denom.reshape(1),
        tile_cols,
    )
    prediction = pred_rows[edge : edge + tile_cols, 2 * edge : 2 * edge + tile_rows].T
    error_sum = jnp.sum(error_lanes)
    grad_band = jnp.transpose(
        grad_taps.reshape(3, second_channels, 3, second_channels), (0, 2, 1, 3)
    ).reshape(9, second_channels, second_channels)
    near_grad = near_lanes[:, 2 * edge : 2 * edge + tile_rows]
    far_grad = far_lanes[:, 5 * edge : 5 * edge + tile_rows + tile_cols - 1]
    enc_start = lax.axis_index("enc") * encoder_bins
    buffer = jnp.zeros((2, second_channels, sequence_length + window_extent), jnp.float32)
    buffer = lax.dynamic_update_slice(buffer, near_grad[None], (0, 0, row_start))
    buffer = lax.dynamic_update_slice(buffer, far_grad[None], (1, 0, row_start + offs_start))
    buffer = buffer[:, :, :sequence_length]
    grad_whole, grad_conv_two, total_error = lax.psum(
        (buffer, grad_band, error_sum), ("enc", "bin", "off")
    )
    grad_embed = lax.dynamic_slice_in_dim(grad_whole, enc_start, encoder_bins, 2).astype(
        jnp.bfloat16
    )
    grad_rows = grad_embed.reshape(2 * second_channels, encoder_bins)
    dhidden = jnp.dot(proj_rows.T, grad_rows, preferred_element_type=jnp.float32).astype(
        jnp.bfloat16
    )
    proj_local = jnp.dot(hidden, grad_rows.T, preferred_element_type=jnp.float32)
    proj_local = jnp.transpose(proj_local.reshape(chans, 2, second_channels), (1, 0, 2))
    conv_local = lax.dot_general(
        dhidden, stacked_enc, (((1,), (1,)), ((), ())), preferred_element_type=jnp.float32
    )
    conv_local = jnp.transpose(conv_local.reshape(chans, 3, width_in), (1, 0, 2))
    grad_proj = lax.psum(proj_local, "enc")
    grad_conv_one = lax.psum_scatter(conv_local, "enc", scatter_dimension=2, tiled=True)
    loss_mean = (total_error / denom).reshape(1)
    return (prediction, loss_mean, grad_conv_two, grad_proj, grad_conv_one)


def solution(mesh):
    in_specs = (
        P(("bin", "off"), "enc"),
        P(("bin", "off")),
        P(None, ("bin", "off"), None),
        P(None, ("bin", "off"), None),
        P(),
        P(),
        P("bin", ("enc", "off")),
        P(),
        P(),
        P(),
    )
    out_specs = (
        P("bin", ("enc", "off")),
        P(),
        P(),
        P(None, ("bin", "off"), None),
        P(None, ("bin", "off"), "enc"),
    )
    return jax.shard_map(shards, mesh=mesh, in_specs=in_specs, out_specs=out_specs, check_vma=False)
```

```python
import functools

import jax
import jax.numpy as jnp
from jax import lax
from jax.experimental import pallas as pl
from jax.experimental.pallas import tpu as pltpu
from jax.sharding import PartitionSpec as P

LARGEST_DILATION = 8


def with_halo(cells, sides, width):
    for axis, dim in sides:
        count = lax.axis_size(axis)
        ends = count - 1
        head = lax.slice_in_dim(cells, 0, width, axis=dim)
        tail = lax.slice_in_dim(cells, cells.shape[dim] - width, cells.shape[dim], axis=dim)
        cells = jnp.concatenate(
            [
                lax.ppermute(tail, axis, [(i, (i + 1) % count) for i in range(ends)]),
                cells,
                lax.ppermute(head, axis, [((i + 1) % count, i) for i in range(ends)]),
            ],
            axis=dim,
        )
    return cells


def count_cells(valid_bins, offset_limit):
    sequence_length = valid_bins.shape[0]
    places = jnp.arange(sequence_length, dtype=jnp.int32)
    gap = places[None, :] - places[:, None]
    scored = (gap >= 0) & (gap < offset_limit[:, None])
    inside = jnp.sum(jnp.where(scored, valid_bins[None, :], 0), axis=1)
    return jnp.sum(valid_bins * inside).astype(jnp.float32)


def place_of(enc_index, group_index, offs):
    return (enc_index, group_index // offs, lax.rem(group_index, offs))


def each(count, body):
    def step(index, carry):
        body(index)
        return carry

    lax.fori_loop(0, count, step, 0)


def push(src, dst, send_sem, recv_sem, where):
    return pltpu.make_async_remote_copy(
        src_ref=src,
        dst_ref=dst,
        send_sem=send_sem,
        recv_sem=recv_sem,
        device_id=where,
        device_id_type=pl.DeviceIdType.MESH,
    )


def greet(where):
    pl.semaphore_signal(
        pltpu.get_barrier_semaphore(), inc=1, device_id=where, device_id_type=pl.DeviceIdType.MESH
    )


def gather_body(encs, bins, offs, x_ref, out_ref, send_group, recv_group, send_edge, recv_edge):
    group = bins * offs
    side = 128
    span = x_ref.shape[1]
    z = lax.axis_index("enc")
    g = lax.axis_index("bin") * offs + lax.axis_index("off")

    def peer(k):
        return lax.rem(g + k + 1, group)

    each(group - 1, lambda k: greet(place_of(z, peer(k), offs)))

    @pl.when(z > 0)
    def _():
        each(group, lambda h: greet(place_of(z - 1, h, offs)))

    @pl.when(z < encs - 1)
    def _():
        each(group, lambda h: greet(place_of(z + 1, h, offs)))

    sides = jnp.minimum(z, 1) + jnp.minimum(encs - 1 - z, 1)
    pl.semaphore_wait(pltpu.get_barrier_semaphore(), group - 1 + group * sides)

    def middle(k, owner):
        return push(
            x_ref,
            out_ref.at[owner, :, pl.ds(side, span)],
            send_group.at[k],
            recv_group.at[owner],
            place_of(z, peer(k), offs),
        )

    def to_left(h, owner):
        return push(
            x_ref.at[:, pl.ds(0, side)],
            out_ref.at[owner, :, pl.ds(side + span, side)],
            send_edge.at[0, h],
            recv_edge.at[0, owner],
            place_of(z - 1, h, offs),
        )

    def to_right(h, owner):
        return push(
            x_ref.at[:, pl.ds(span - side, side)],
            out_ref.at[owner, :, pl.ds(0, side)],
            send_edge.at[1, h],
            recv_edge.at[1, owner],
            place_of(z + 1, h, offs),
        )

    each(group - 1, lambda k: middle(k, g).start())

    @pl.when(z > 0)
    def _():
        each(group, lambda h: to_left(h, g).start())

    @pl.when(z < encs - 1)
    def _():
        each(group, lambda h: to_right(h, g).start())

    out_ref[g, :, side : side + span] = x_ref[...]
    blank = jnp.zeros((group, x_ref.shape[0], side), x_ref.dtype)

    @pl.when(z == 0)
    def _():
        out_ref[:, :, :side] = blank

    @pl.when(z == encs - 1)
    def _():
        out_ref[:, :, side + span :] = blank

    def settle(k):
        middle(k, g).wait_send()
        middle(k, peer(k)).wait_recv()

    each(group - 1, settle)

    @pl.when(z > 0)
    def _():
        def settle_left(h):
            to_left(h, g).wait_send()
            to_right(h, h).wait_recv()

        each(group, settle_left)

    @pl.when(z < encs - 1)
    def _():
        def settle_right(h):
            to_right(h, g).wait_send()
            to_left(h, h).wait_recv()

        each(group, settle_right)


def gather_framed(x, encs, bins, offs):
    group = bins * offs
    vmem = pl.BlockSpec(memory_space=pltpu.VMEM)
    return pl.pallas_call(
        functools.partial(gather_body, encs, bins, offs),
        out_shape=jax.ShapeDtypeStruct((group, x.shape[0], x.shape[1] + 256), x.dtype),
        in_specs=[vmem],
        out_specs=vmem,
        scratch_shapes=[
            pltpu.SemaphoreType.DMA((group,)),
            pltpu.SemaphoreType.DMA((group,)),
            pltpu.SemaphoreType.DMA((2, group)),
            pltpu.SemaphoreType.DMA((2, group)),
        ],
        compiler_params=pltpu.CompilerParams(collective_id=0, has_side_effects=True),
        name="gather_framed",
    )(x)


def exchange_body(
    encs, bins, offs, spread, x_ref, out_ref, slots, total, lines, sends, recvs, line_sends, line_recvs
):
    group = bins * offs
    z = lax.axis_index("enc")
    g = lax.axis_index("bin") * offs + lax.axis_index("off")

    def peer(k):
        return lax.rem(g + k + 1, group)

    def line(k):
        return lax.rem(z + k + 1, encs)

    def in_group(k):
        return place_of(z, peer(k), offs)

    def in_line(k):
        return place_of(line(k), g, offs)

    each(group - 1, lambda k: greet(in_group(k)))
    each(encs - 1, lambda k: greet(in_line(k)))
    pl.semaphore_wait(pltpu.get_barrier_semaphore(), group + encs - 2)

    def split(k, owner):
        return push(
            x_ref.at[peer(k)], slots.at[owner], sends.at[0, k], recvs.at[0, owner], in_group(k)
        )

    each(group - 1, lambda k: split(k, g).start())
    slots[g] = x_ref[g]

    def settle_split(k):
        split(k, g).wait_send()
        split(k, peer(k)).wait_recv()

    each(group - 1, settle_split)
    summed = slots[0]
    for h in range(1, group):
        summed = summed + slots[h]
    if spread:
        total[...] = summed

        def across(k, owner, part):
            return push(
                total.at[encs if part else line(k)],
                lines.at[owner, part],
                line_sends.at[part, k],
                line_recvs.at[part, owner],
                in_line(k),
            )

        def begin_across(k):
            for part in range(2):
                across(k, z, part).start()

        each(encs - 1, begin_across)
        lines[z, 0] = total[z]
        lines[z, 1] = total[encs]

        def settle_across(k):
            for part in range(2):
                across(k, z, part).wait_send()
                across(k, line(k), part).wait_recv()

        each(encs - 1, settle_across)
        piece = lines[0, 0]
        shared = lines[0, 1]
        for other in range(1, encs):
            piece = piece + lines[other, 0]
            shared = shared + lines[other, 1]
        out_ref[g, encs] = shared
    else:
        piece = summed[0]
    out_ref[g, z] = piece.astype(jnp.bfloat16).astype(jnp.float32)

    def along(k, owner):
        return push(
            out_ref.at[g, z],
            out_ref.at[g, owner],
            line_sends.at[2, k],
            line_recvs.at[2, owner],
            in_line(k),
        )

    each(encs - 1, lambda k: along(k, z).start())

    def settle_along(k):
        along(k, z).wait_send()
        along(k, line(k)).wait_recv()

    each(encs - 1, settle_along)

    def spread_out(k, owner):
        return push(
            out_ref.at[g], out_ref.at[owner], sends.at[1, k], recvs.at[1, owner], in_group(k)
        )

    each(group - 1, lambda k: spread_out(k, g).start())

    def settle_out(k):
        spread_out(k, g).wait_send()
        spread_out(k, peer(k)).wait_recv()

    each(group - 1, settle_out)


def exchange(x, encs, bins, offs, spread, ident, name):
    group, parts, rows, span = x.shape
    vmem = pl.BlockSpec(memory_space=pltpu.VMEM)
    return pl.pallas_call(
        functools.partial(exchange_body, encs, bins, offs, spread),
        out_shape=jax.ShapeDtypeStruct((group, encs + int(spread), rows, span), jnp.float32),
        in_specs=[vmem],
        out_specs=vmem,
        scratch_shapes=[
            pltpu.VMEM((group, parts, rows, span), jnp.float32),
            pltpu.VMEM((parts, rows, span), jnp.float32),
            pltpu.VMEM((encs, 2, rows, span), jnp.float32),
            pltpu.SemaphoreType.DMA((2, group)),
            pltpu.SemaphoreType.DMA((2, group)),
            pltpu.SemaphoreType.DMA((3, encs)),
            pltpu.SemaphoreType.DMA((3, encs)),
        ],
        compiler_params=pltpu.CompilerParams(collective_id=ident, has_side_effects=True),
        name=name,
    )(x)


def round_up(value, step):
    return (value + step - 1) // step * step


def band_body(
    edge,
    rows,
    unroll,
    dil_ref,
    place_ref,
    denom_ref,
    near_ref,
    far_ref,
    fmask_ref,
    lanes_ref,
    limit_ref,
    target_ref,
    head_ref,
    wfwd_ref,
    wback_ref,
    pred_ref,
    err_ref,
    gband_ref,
    gnear_ref,
    gfar_ref,
    far_rolled,
    mask_rolled,
    near_shift,
    stack,
    resid_acc,
    dact_acc,
    own_grad,
):
    chans, width = near_ref.shape
    wide = far_ref.shape[1]
    d = dil_ref[0]
    offs_first = place_ref[0]
    offs_count = place_ref[1]
    denom = denom_ref[0]
    all_rows = rows + 4 * edge
    last = rows + 3 * edge

    def loop(start, stop, body, init):
        def step(index, carry):
            for inner in range(unroll):
                carry = body(start + index * unroll + inner, carry)
            return carry

        return lax.fori_loop(0, (stop - start) // unroll, step, init)

    near_shift[1] = near_ref[...]
    near_shift[0] = pltpu.roll(near_ref[...], d, 1)
    near_shift[2] = pltpu.roll(near_ref[...], width - d, 1)

    def fill(k, carry):
        shift = lax.rem(wide - k, wide)
        far_rolled[k] = pltpu.roll(far_ref[...], shift, 1)[:, :width].astype(jnp.bfloat16)
        mask_rolled[k] = pltpu.roll(fmask_ref[...], shift, 1)[:, :width]
        return carry

    loop(0, all_rows + 2 * edge, fill, 0)

    def clear(r, carry):
        resid_acc[r + edge] = near_ref[...] + far_rolled[r + edge].astype(jnp.float32)
        dact_acc[r] = jnp.zeros((chans, width), jnp.float32)
        return carry

    loop(0, all_rows, clear, 0)
    for r in list(range(edge)) + list(range(last, all_rows)):
        own_grad[r] = jnp.zeros((chans, width), jnp.bfloat16)

    def forward(r, carry):
        offs = offs_first + r - 2 * edge
        inside = jnp.where((offs >= 0) & (offs < offs_count), 1.0, 0.0)
        for a in range(3):
            cells = near_shift[a] + far_rolled[r + edge + (a - 1) * d].astype(jnp.float32)
            cells = jnp.maximum(cells, 0.0) * inside
            stack[r, a * chans : (a + 1) * chans, :] = cells.astype(jnp.bfloat16)
        taps = jnp.dot(wfwd_ref[...], stack[r], preferred_element_type=jnp.float32)
        for b in range(3):
            spot = r + edge - (b - 1) * d
            resid_acc[spot] = resid_acc[spot] + taps[b * chans : (b + 1) * chans]
        return carry

    loop(0, all_rows, forward, 0)

    def middle(r, err):
        resid = resid_acc[r + edge]
        head = head_ref[...]
        pred = jnp.sum(head * jnp.maximum(resid, 0.0), axis=0, keepdims=True)
        pred_ref[pl.ds(r - edge, 1), :] = pred
        offs = offs_first + r - 2 * edge
        inside = jnp.where((offs >= 0) & (offs < offs_count), 1.0, 0.0)
        own_row = jnp.where((r >= 2 * edge) & (r < rows + 2 * edge), 1.0, 0.0)
        weight = (
            lanes_ref[0:1, :]
            * mask_rolled[r + edge][0:1, :]
            * jnp.where(offs < limit_ref[...], inside, 0.0)
        )
        differ = pred - target_ref[pl.ds(r - edge, 1), :]
        own = lanes_ref[1:2, :] * own_row
        err = err + weight * differ * differ * own
        dpred = 2.0 * weight * differ / denom
        dres = jnp.where(resid > 0.0, head * dpred, 0.0).astype(jnp.bfloat16).astype(jnp.float32)
        own_grad[r] = (dres * own).astype(jnp.bfloat16)
        shifted = jnp.concatenate(
            [
                pltpu.roll(dres, width - d, 1).astype(jnp.bfloat16),
                dres.astype(jnp.bfloat16),
                pltpu.roll(dres, d, 1).astype(jnp.bfloat16),
            ],
            axis=0,
        )
        taps = jnp.dot(wback_ref[...], shifted, preferred_element_type=jnp.float32)
        for b in range(3):
            spot = r + (b - 1) * d
            dact_acc[spot] = dact_acc[spot] + taps[b * chans : (b + 1) * chans]
        return err

    err = loop(edge, last, middle, jnp.zeros((1, width), jnp.float32))
    err_ref[...] = err

    def weigh(r, total):
        grads = jnp.concatenate([own_grad[r - (b - 1) * d] for b in range(3)], axis=0)
        return total + lax.dot_general(
            stack[r], grads, (((1,), (1,)), ((), ())), preferred_element_type=jnp.float32
        )

    gband_ref[...] = loop(edge, last, weigh, jnp.zeros((3 * chans, 3 * chans), jnp.float32))

    own_near = jnp.where(lanes_ref[1:2, :] > 0.0, near_ref[...], -jnp.inf)
    gnear_ref[...] = jnp.zeros(gnear_ref.shape, jnp.float32)
    gfar_ref[...] = jnp.zeros(gfar_ref.shape, jnp.float32)
    blank = jnp.zeros((chans, wide - width), jnp.float32)
    near_shift[0] = own_near

    def collect(r, carry):
        pair = near_shift[0] + far_rolled[r + edge].astype(jnp.float32)
        dpair = own_grad[r].astype(jnp.float32) + jnp.where(pair > 0.0, dact_acc[r], 0.0)
        gnear_ref[...] += dpair
        gfar_ref[...] += pltpu.roll(jnp.concatenate([dpair, blank], axis=1), r + edge, 1)
        return carry

    loop(2 * edge, rows + 2 * edge, collect, 0)


def band(near, far, fmask, lanes, limits, target, head, wfwd, wback, dil, place, denom, rows):
    chans, width = near.shape
    wide = far.shape[1]
    edge = LARGEST_DILATION
    all_rows = rows + 4 * edge
    smem = pl.BlockSpec(memory_space=pltpu.SMEM)
    vmem = pl.BlockSpec(memory_space=pltpu.VMEM)
    return pl.pallas_call(
        functools.partial(band_body, edge, rows, 4),
        out_shape=(
            jax.ShapeDtypeStruct((rows + 2 * edge, width), jnp.float32),
            jax.ShapeDtypeStruct((1, width), jnp.float32),
            jax.ShapeDtypeStruct((3 * chans, 3 * chans), jnp.float32),
            jax.ShapeDtypeStruct((chans, width), jnp.float32),
            jax.ShapeDtypeStruct((chans, wide), jnp.float32),
        ),
        in_specs=[smem] * 3 + [vmem] * 9,
        out_specs=(vmem,) * 5,
        scratch_shapes=[
            pltpu.VMEM((all_rows + 2 * edge, chans, width), jnp.bfloat16),
            pltpu.VMEM((all_rows + 2 * edge, 8, width), jnp.float32),
            pltpu.VMEM((3, chans, width), jnp.float32),
            pltpu.VMEM((all_rows, 3 * chans, width), jnp.bfloat16),
            pltpu.VMEM((all_rows + 2 * edge, chans, width), jnp.float32),
            pltpu.VMEM((all_rows, chans, width), jnp.float32),
            pltpu.VMEM((all_rows, chans, width), jnp.bfloat16),
        ],
        compiler_params=pltpu.CompilerParams(vmem_limit_bytes=60 * 1024 * 1024),
        cost_estimate=pl.CostEstimate(flops=4000000000, bytes_accessed=2000000, transcendentals=0),
        name="band",
    )(dil, place, denom, near, far, fmask, lanes, limits, target, head, wfwd, wback)


def shards(
    encoder_in,
    gain_enc,
    conv_one,
    proj_weight,
    conv_two,
    head_weight,
    target,
    valid_bins,
    offset_limit,
    dilations,
):
    chans, encoder_bins = encoder_in.shape
    width_in = conv_one.shape[2]
    second_channels = conv_two.shape[1]
    tile_rows, tile_cols = target.shape
    first_dilation = dilations[0]
    second_dilation = dilations[1]
    activ = jax.nn.gelu(gain_enc[:, None] * encoder_in.astype(jnp.float32)).astype(jnp.bfloat16)
    encs, bins, offs = (lax.axis_size(axis) for axis in ("enc", "bin", "off"))
    group = bins * offs
    rows_piece = 2 * second_channels // group
    framed = gather_framed(activ, encs, bins, offs).reshape(width_in, encoder_bins + 256)
    stacked_enc = jnp.concatenate(
        [
            lax.dynamic_slice_in_dim(framed, 128 + (tap - 1) * first_dilation, encoder_bins, 1)
            for tap in range(3)
        ],
        axis=0,
    )
    weight_one = jnp.transpose(conv_one, (1, 0, 2)).reshape(chans, 3 * width_in)
    conv_out = jnp.dot(weight_one, stacked_enc, preferred_element_type=jnp.float32)
    hidden = (encoder_in.astype(jnp.float32) + conv_out).astype(jnp.bfloat16)
    proj_rows = jnp.transpose(proj_weight, (0, 2, 1)).reshape(2 * second_channels, chans)
    partial_embed = jnp.dot(proj_rows, hidden, preferred_element_type=jnp.float32)
    pieces = exchange(
        partial_embed.reshape(group, 1, rows_piece, encoder_bins), encs, bins, offs, False, 1, "embed"
    )
    embed = jnp.transpose(pieces, (0, 2, 1, 3)).reshape(2 * second_channels, encs * encoder_bins)
    enc_index = lax.axis_index("enc")
    share = width_in // encs

    def parcel(owner):
        rows = lax.dynamic_slice(framed, (owner * share, 128), (share, encoder_bins))
        return jnp.concatenate([rows, hidden], axis=0)

    whole_side = jnp.zeros((share + chans, encs * encoder_bins), jnp.bfloat16)
    whole_side = lax.dynamic_update_slice(
        whole_side, parcel(enc_index), (0, enc_index * encoder_bins)
    )
    for hop in range(1, encs):
        arrived = lax.ppermute(
            parcel(lax.rem(enc_index + hop, encs)),
            "enc",
            [(i, (i + hop) % encs) for i in range(encs)],
        )
        origin = lax.rem(enc_index + encs - hop, encs)
        whole_side = lax.dynamic_update_slice(whole_side, arrived, (0, origin * encoder_bins))
    sequence_length = embed.shape[1]
    window_extent = tile_cols * encs * offs
    row_start = lax.axis_index("bin") * tile_rows
    offs_start = (lax.axis_index("enc") * lax.axis_size("off") + lax.axis_index("off")) * tile_cols
    edge = LARGEST_DILATION
    width = round_up(tile_rows + 4 * edge, 128)
    wide = round_up(tile_rows + tile_cols + 10 * edge, 128)
    bin_ids = row_start - 2 * edge + jnp.arange(width, dtype=jnp.int32)
    inside = (bin_ids >= 0) & (bin_ids < sequence_length)
    near = lax.dynamic_slice_in_dim(
        jnp.pad(embed[:second_channels], ((0, 0), (2 * edge, width))),
        row_start,
        width,
        1,
    )
    near = jnp.where(inside[None, :], near, -jnp.inf)
    far = lax.dynamic_slice_in_dim(
        jnp.pad(
            embed[second_channels:], ((0, 0), (5 * edge, window_extent + wide))
        ),
        row_start + offs_start,
        wide,
        1,
    )
    mask_float = valid_bins.astype(jnp.float32)
    far_mask = lax.dynamic_slice_in_dim(
        jnp.pad(mask_float, (5 * edge, window_extent + wide)), row_start + offs_start, wide
    )
    near_mask = lax.dynamic_slice_in_dim(
        jnp.pad(mask_float, (2 * edge, width)), row_start, width
    )
    limits = lax.dynamic_slice_in_dim(jnp.pad(offset_limit, (2 * edge, width)), row_start, width)
    spots = jnp.arange(width, dtype=jnp.int32)
    framed_lane = (spots >= edge) & (spots < tile_rows + 3 * edge)
    own_lane = (spots >= 2 * edge) & (spots < tile_rows + 2 * edge)
    lanes = jnp.stack([jnp.where(framed_lane, near_mask, 0.0), own_lane.astype(jnp.float32)])
    lanes = jnp.pad(lanes, ((0, 6), (0, 0)))
    denom = 1.0 + count_cells(valid_bins, offset_limit)
    framed_target = with_halo(target, (("bin", 0), (("enc", "off"), 1)), edge)
    target_rows = jnp.pad(
        framed_target.T.astype(jnp.float32), ((0, 0), (edge, width - tile_rows - 3 * edge))
    )
    taps = conv_two.reshape(3, 3, second_channels, second_channels)
    weight_fwd = jnp.transpose(taps, (1, 3, 0, 2)).reshape(3 * second_channels, 3 * second_channels)
    weight_back = jnp.transpose(taps, (1, 2, 0, 3)).reshape(3 * second_channels, 3 * second_channels)
    pred_rows, error_lanes, grad_taps, near_lanes, far_lanes = band(
        near,
        far,
        jnp.broadcast_to(far_mask[None, :], (8, wide)),
        lanes,
        limits[None, :],
        target_rows,
        jnp.broadcast_to(head_weight[:, None], (second_channels, width)),
        weight_fwd,
        weight_back,
        second_dilation.reshape(1),
        jnp.stack([offs_start, jnp.full((), window_extent, jnp.int32)]).astype(jnp.int32),
        denom.reshape(1),
        tile_cols,
    )
    prediction = pred_rows[edge : edge + tile_cols, 2 * edge : 2 * edge + tile_rows].T
    near_grad = near_lanes[:, 2 * edge : 2 * edge + tile_rows]
    far_grad = far_lanes[:, 5 * edge : 5 * edge + tile_rows + tile_cols - 1]
    buffer = jnp.zeros((2 * second_channels, sequence_length + window_extent), jnp.float32)
    buffer = lax.dynamic_update_slice(buffer, near_grad, (0, row_start))
    buffer = lax.dynamic_update_slice(buffer, far_grad, (second_channels, row_start + offs_start))
    buffer = buffer[:, :sequence_length].reshape(group, rows_piece, encs, encoder_bins)
    taps_rows, error_rows = grad_taps.shape[0], width // 128
    half = 2 * second_channels
    common = jnp.concatenate(
        [
            jnp.pad(grad_taps, ((0, 0), (0, 128 - taps_rows))),
            error_lanes.reshape(error_rows, 128),
            jnp.zeros((2 * half - taps_rows - error_rows, 128), jnp.float32),
        ]
    )
    common = jnp.transpose(common.reshape(group, 2, rows_piece, 128), (0, 2, 1, 3))
    common = common.reshape(group, 1, rows_piece, 256)
    common = jnp.pad(common, ((0, 0), (0, 0), (0, 0), (0, encoder_bins - 256)))
    outgoing = jnp.concatenate([jnp.transpose(buffer, (0, 2, 1, 3)), common], axis=1)
    summed = exchange(outgoing, encs, bins, offs, True, 2, "grads")
    grad_rows = jnp.transpose(summed[:, :encs], (0, 2, 1, 3)).reshape(half, sequence_length)
    grad_rows = grad_rows.astype(jnp.bfloat16)
    common = summed[:, encs, :, :256].reshape(group, rows_piece, 2, 128)
    common = jnp.transpose(common, (0, 2, 1, 3)).reshape(2 * half, 128)
    grad_conv_two = jnp.transpose(
        common[:taps_rows, :taps_rows].reshape(3, second_channels, 3, second_channels), (0, 2, 1, 3)
    ).reshape(9, second_channels, second_channels)
    total_error = jnp.sum(common[taps_rows : taps_rows + error_rows])
    dhidden = jnp.dot(proj_rows.T, grad_rows, preferred_element_type=jnp.float32).astype(
        jnp.bfloat16
    )
    activ_side = jnp.pad(whole_side[:share], ((0, 0), (edge, edge)))
    hidden_side = whole_side[share:]
    across = (((1,), (1,)), ((), ()))
    grad_proj = lax.dot_general(
        hidden_side, grad_rows, across, preferred_element_type=jnp.float32
    )
    grad_proj = jnp.stack([grad_proj[:, :second_channels], grad_proj[:, second_channels:]])
    grad_conv_one = jnp.stack(
        [
            lax.dot_general(
                dhidden,
                lax.dynamic_slice_in_dim(
                    activ_side, edge + (tap - 1) * first_dilation, sequence_length, 1
                ),
                across,
                preferred_element_type=jnp.float32,
            )
            for tap in range(3)
        ]
    )
    loss_mean = (total_error / denom).reshape(1)
    return (prediction, loss_mean, grad_conv_two, grad_proj, grad_conv_one)


def solution(mesh):
    in_specs = (
        P(("bin", "off"), "enc"),
        P(("bin", "off")),
        P(None, ("bin", "off"), None),
        P(None, ("bin", "off"), None),
        P(),
        P(),
        P("bin", ("enc", "off")),
        P(),
        P(),
        P(),
    )
    out_specs = (
        P("bin", ("enc", "off")),
        P(),
        P(),
        P(None, ("bin", "off"), None),
        P(None, ("bin", "off"), "enc"),
    )
    return jax.shard_map(shards, mesh=mesh, in_specs=in_specs, out_specs=out_specs, check_vma=False)
```

```python
import functools

import jax
import jax.numpy as jnp
from jax import lax
from jax.experimental import pallas as pl
from jax.experimental.pallas import tpu as pltpu
from jax.sharding import PartitionSpec as P

LARGEST_DILATION = 8


def with_halo(cells, sides, width):
    for axis, dim in sides:
        count = lax.axis_size(axis)
        ends = count - 1
        head = lax.slice_in_dim(cells, 0, width, axis=dim)
        tail = lax.slice_in_dim(cells, cells.shape[dim] - width, cells.shape[dim], axis=dim)
        cells = jnp.concatenate(
            [
                lax.ppermute(tail, axis, [(i, (i + 1) % count) for i in range(ends)]),
                cells,
                lax.ppermute(head, axis, [((i + 1) % count, i) for i in range(ends)]),
            ],
            axis=dim,
        )
    return cells


def count_cells(valid_bins, offset_limit):
    sequence_length = valid_bins.shape[0]
    places = jnp.arange(sequence_length, dtype=jnp.int32)
    gap = places[None, :] - places[:, None]
    scored = (gap >= 0) & (gap < offset_limit[:, None])
    inside = jnp.sum(jnp.where(scored, valid_bins[None, :], 0), axis=1)
    return jnp.sum(valid_bins * inside).astype(jnp.float32)


def place_of(enc_index, group_index, offs):
    return (enc_index, group_index // offs, lax.rem(group_index, offs))


def each(count, body):
    def step(index, carry):
        body(index)
        return carry

    lax.fori_loop(0, count, step, 0)


def push(src, dst, send_sem, recv_sem, where):
    return pltpu.make_async_remote_copy(
        src_ref=src,
        dst_ref=dst,
        send_sem=send_sem,
        recv_sem=recv_sem,
        device_id=where,
        device_id_type=pl.DeviceIdType.MESH,
    )


def greet(where):
    pl.semaphore_signal(
        pltpu.get_barrier_semaphore(), inc=1, device_id=where, device_id_type=pl.DeviceIdType.MESH
    )


def gather_body(encs, bins, offs, x_ref, out_ref, send_group, recv_group, send_edge, recv_edge):
    group = bins * offs
    side = 128
    span = x_ref.shape[1]
    z = lax.axis_index("enc")
    g = lax.axis_index("bin") * offs + lax.axis_index("off")

    def peer(k):
        return lax.rem(g + k + 1, group)

    each(group - 1, lambda k: greet(place_of(z, peer(k), offs)))

    @pl.when(z > 0)
    def _():
        each(group, lambda h: greet(place_of(z - 1, h, offs)))

    @pl.when(z < encs - 1)
    def _():
        each(group, lambda h: greet(place_of(z + 1, h, offs)))

    sides = jnp.minimum(z, 1) + jnp.minimum(encs - 1 - z, 1)
    pl.semaphore_wait(pltpu.get_barrier_semaphore(), group - 1 + group * sides)

    def middle(k, owner):
        return push(
            x_ref,
            out_ref.at[owner, :, pl.ds(side, span)],
            send_group.at[k],
            recv_group.at[owner],
            place_of(z, peer(k), offs),
        )

    def to_left(h, owner):
        return push(
            x_ref.at[:, pl.ds(0, side)],
            out_ref.at[owner, :, pl.ds(side + span, side)],
            send_edge.at[0, h],
            recv_edge.at[0, owner],
            place_of(z - 1, h, offs),
        )

    def to_right(h, owner):
        return push(
            x_ref.at[:, pl.ds(span - side, side)],
            out_ref.at[owner, :, pl.ds(0, side)],
            send_edge.at[1, h],
            recv_edge.at[1, owner],
            place_of(z + 1, h, offs),
        )

    each(group - 1, lambda k: middle(k, g).start())

    @pl.when(z > 0)
    def _():
        each(group, lambda h: to_left(h, g).start())

    @pl.when(z < encs - 1)
    def _():
        each(group, lambda h: to_right(h, g).start())

    out_ref[g, :, side : side + span] = x_ref[...]
    blank = jnp.zeros((group, x_ref.shape[0], side), x_ref.dtype)

    @pl.when(z == 0)
    def _():
        out_ref[:, :, :side] = blank

    @pl.when(z == encs - 1)
    def _():
        out_ref[:, :, side + span :] = blank

    def settle(k):
        middle(k, g).wait_send()
        middle(k, peer(k)).wait_recv()

    each(group - 1, settle)

    @pl.when(z > 0)
    def _():
        def settle_left(h):
            to_left(h, g).wait_send()
            to_right(h, h).wait_recv()

        each(group, settle_left)

    @pl.when(z < encs - 1)
    def _():
        def settle_right(h):
            to_right(h, g).wait_send()
            to_left(h, h).wait_recv()

        each(group, settle_right)


def gather_framed(x, encs, bins, offs):
    group = bins * offs
    vmem = pl.BlockSpec(memory_space=pltpu.VMEM)
    return pl.pallas_call(
        functools.partial(gather_body, encs, bins, offs),
        out_shape=jax.ShapeDtypeStruct((group, x.shape[0], x.shape[1] + 256), x.dtype),
        in_specs=[vmem],
        out_specs=vmem,
        scratch_shapes=[
            pltpu.SemaphoreType.DMA((group,)),
            pltpu.SemaphoreType.DMA((group,)),
            pltpu.SemaphoreType.DMA((2, group)),
            pltpu.SemaphoreType.DMA((2, group)),
        ],
        compiler_params=pltpu.CompilerParams(collective_id=0, has_side_effects=True),
        name="gather_framed",
    )(x)


def exchange_body(
    encs, bins, offs, spread, x_ref, out_ref, slots, total, lines, sends, recvs, line_sends, line_recvs
):
    group = bins * offs
    z = lax.axis_index("enc")
    g = lax.axis_index("bin") * offs + lax.axis_index("off")

    def peer(k):
        return lax.rem(g + k + 1, group)

    def line(k):
        return lax.rem(z + k + 1, encs)

    def in_group(k):
        return place_of(z, peer(k), offs)

    def in_line(k):
        return place_of(line(k), g, offs)

    each(group - 1, lambda k: greet(in_group(k)))
    each(encs - 1, lambda k: greet(in_line(k)))
    pl.semaphore_wait(pltpu.get_barrier_semaphore(), group + encs - 2)

    def split(k, owner):
        return push(
            x_ref.at[peer(k)], slots.at[owner], sends.at[0, k], recvs.at[0, owner], in_group(k)
        )

    each(group - 1, lambda k: split(k, g).start())
    slots[g] = x_ref[g]

    def settle_split(k):
        split(k, g).wait_send()
        split(k, peer(k)).wait_recv()

    each(group - 1, settle_split)
    summed = slots[0]
    for h in range(1, group):
        summed = summed + slots[h]
    if spread:
        total[...] = summed

        def across(k, owner, part):
            return push(
                total.at[encs if part else line(k)],
                lines.at[owner, part],
                line_sends.at[part, k],
                line_recvs.at[part, owner],
                in_line(k),
            )

        def begin_across(k):
            for part in range(2):
                across(k, z, part).start()

        each(encs - 1, begin_across)
        lines[z, 0] = total[z]
        lines[z, 1] = total[encs]

        def settle_across(k):
            for part in range(2):
                across(k, z, part).wait_send()
                across(k, line(k), part).wait_recv()

        each(encs - 1, settle_across)
        piece = lines[0, 0]
        shared = lines[0, 1]
        for other in range(1, encs):
            piece = piece + lines[other, 0]
            shared = shared + lines[other, 1]
        out_ref[g, encs] = shared
    else:
        piece = summed[0]
    out_ref[g, z] = piece.astype(jnp.bfloat16).astype(jnp.float32)

    def along(k, owner):
        return push(
            out_ref.at[g, z],
            out_ref.at[g, owner],
            line_sends.at[2, k],
            line_recvs.at[2, owner],
            in_line(k),
        )

    each(encs - 1, lambda k: along(k, z).start())

    def settle_along(k):
        along(k, z).wait_send()
        along(k, line(k)).wait_recv()

    each(encs - 1, settle_along)

    def spread_out(k, owner):
        return push(
            out_ref.at[g], out_ref.at[owner], sends.at[1, k], recvs.at[1, owner], in_group(k)
        )

    each(group - 1, lambda k: spread_out(k, g).start())

    def settle_out(k):
        spread_out(k, g).wait_send()
        spread_out(k, peer(k)).wait_recv()

    each(group - 1, settle_out)


def exchange(x, encs, bins, offs, spread, ident, name):
    group, parts, rows, span = x.shape
    vmem = pl.BlockSpec(memory_space=pltpu.VMEM)
    return pl.pallas_call(
        functools.partial(exchange_body, encs, bins, offs, spread),
        out_shape=jax.ShapeDtypeStruct((group, encs + int(spread), rows, span), jnp.float32),
        in_specs=[vmem],
        out_specs=vmem,
        scratch_shapes=[
            pltpu.VMEM((group, parts, rows, span), jnp.float32),
            pltpu.VMEM((parts, rows, span), jnp.float32),
            pltpu.VMEM((encs, 2, rows, span), jnp.float32),
            pltpu.SemaphoreType.DMA((2, group)),
            pltpu.SemaphoreType.DMA((2, group)),
            pltpu.SemaphoreType.DMA((3, encs)),
            pltpu.SemaphoreType.DMA((3, encs)),
        ],
        compiler_params=pltpu.CompilerParams(collective_id=ident, has_side_effects=True),
        name=name,
    )(x)


def round_up(value, step):
    return (value + step - 1) // step * step


RING = 32
UNROLL = 4


def band_body(
    edge,
    rows,
    dil_ref,
    place_ref,
    denom_ref,
    embed_ref,
    bins_ref,
    target_ref,
    head_ref,
    taps_ref,
    pred_ref,
    err_ref,
    gband_ref,
    gnear_ref,
    gfar_ref,
    near_ext,
    far_ext,
    far_rolled,
    mask_rolled,
    near_shift,
    near_own,
    stack,
    sums,
    backs,
    own_grad,
    block,
):
    group, encs, rows_piece, span = embed_ref.shape
    chans = head_ref.shape[0]
    width = gnear_ref.shape[1]
    wide = gfar_ref.shape[1]
    lag = edge + UNROLL
    d = dil_ref[0]
    row_start = pl.multiple_of(place_ref[0], 128)
    offs_first = place_ref[1]
    offs_count = place_ref[2]
    far_start = pl.multiple_of(row_start + offs_first, 128)
    denom = denom_ref[0]
    seq = encs * span

    near_ext[...] = jnp.zeros(near_ext.shape, jnp.float32)
    far_ext[...] = jnp.zeros(far_ext.shape, jnp.float32)
    for g in range(group):
        first = g * rows_piece
        for z in range(encs):
            here = slice(128 + z * span, 128 + (z + 1) * span)
            if first < chans:
                near_ext[first : first + rows_piece, here] = embed_ref[g, z]
            else:
                far_ext[first - chans : first - chans + rows_piece, here] = embed_ref[g, z]
    near_ext[chans : chans + 8, 128 : 128 + seq] = bins_ref[...].astype(jnp.float32)
    far_ext[chans : chans + 8, 128 : 128 + seq] = bins_ref[...].astype(jnp.float32)
    around = near_ext[:, pl.ds(row_start, width + 128)]
    around = pltpu.roll(around, width + 2 * edge, 1)[:, :width]
    ahead = far_ext[:, pl.ds(far_start, wide + 128)]
    ahead = pltpu.roll(ahead, wide + 5 * edge, 1)[:, :wide]
    spots = lax.broadcasted_iota(jnp.int32, (1, width), 1)
    bin_ids = row_start - 2 * edge + spots
    near = jnp.where((bin_ids >= 0) & (bin_ids < seq), around[:chans], -jnp.inf)
    own_lane = (spots >= 2 * edge) & (spots < width - 128 + 2 * edge)
    framed_lane = (spots >= edge) & (spots < width - 128 + 3 * edge)
    scored = jnp.where(framed_lane, around[chans : chans + 1], 0.0)
    limit = around[chans + 1 : chans + 2]
    near_own[0] = near
    near_own[1] = jnp.where(own_lane, near, -jnp.inf)
    near_shift[1] = near.astype(jnp.bfloat16)
    near_shift[0] = pltpu.roll(near, d, 1).astype(jnp.bfloat16)
    near_shift[2] = pltpu.roll(near, width - d, 1).astype(jnp.bfloat16)
    far_ext[:, :wide] = ahead

    block[...] = jnp.zeros(block.shape, jnp.float32)
    for a in range(3):
        for b in range(3):
            tap = taps_ref[3 * a + b].astype(jnp.float32)
            block[0, a * chans : (a + 1) * chans, b * chans : (b + 1) * chans] = tap
            block[1, b * chans : (b + 1) * chans, a * chans : (a + 1) * chans] = tap
    forward_taps = block[0].T[: 3 * chans, : 3 * chans].astype(jnp.bfloat16)
    back_taps = block[1][: 3 * chans, : 3 * chans].astype(jnp.bfloat16)

    def fill(index, carry):
        for u in range(UNROLL):
            k = index * UNROLL + u
            turned = pltpu.roll(far_ext[:, :wide], lax.rem(wide - k, wide), 1)[:, :width]
            far_rolled[k] = turned[:chans].astype(jnp.bfloat16)
            mask_rolled[k] = turned[chans : chans + 8]
        return carry

    total = rows + 6 * edge
    lax.fori_loop(0, (total + 2 * edge) // UNROLL, fill, 0)
    stack[...] = jnp.zeros(stack.shape, jnp.bfloat16)
    own_grad[...] = jnp.zeros(own_grad.shape, jnp.bfloat16)
    gband_ref[...] = jnp.zeros(gband_ref.shape, jnp.float32)
    gnear_ref[...] = jnp.zeros(gnear_ref.shape, jnp.float32)
    gfar_ref[...] = jnp.zeros(gfar_ref.shape, jnp.float32)
    head = head_ref[...]
    blank = jnp.zeros((chans, wide - width), jnp.float32)

    def slot(r):
        return lax.rem(r + 2 * RING, RING)

    def owned(r):
        return (r >= 2 * edge) & (r < rows + 2 * edge)

    def step(index, err):
        start = index * UNROLL
        near_sum = jnp.zeros((chans, width), jnp.float32)
        far_sum = jnp.zeros((chans, wide), jnp.float32)
        cells_old = []
        grads_old = []
        for u in range(UNROLL):
            r = start + u - 2 * lag
            pair = near_own[1] + far_rolled[jnp.maximum(r + edge, 0)].astype(jnp.float32)
            dact = (
                backs[slot(r + d), :chans]
                + backs[slot(r), chans : 2 * chans]
                + backs[slot(r - d), 2 * chans :]
            )
            dpair = own_grad[slot(r)].astype(jnp.float32) + jnp.where(pair > 0.0, dact, 0.0)
            dpair = jnp.where(owned(r), dpair, 0.0)
            near_sum = near_sum + dpair
            far_sum = far_sum + pltpu.roll(
                jnp.concatenate([dpair, blank], axis=1), lax.rem(r + edge + wide, wide), 1
            )
            cells_old.append(stack[slot(r)])
            grads_old.append(
                jnp.concatenate(
                    [own_grad[slot(r + d)], own_grad[slot(r)], own_grad[slot(r - d)]], axis=0
                )
            )
        gnear_ref[...] += near_sum
        gfar_ref[...] += far_sum
        gband_ref[...] += lax.dot_general(
            jnp.concatenate(cells_old, axis=1),
            jnp.concatenate(grads_old, axis=1),
            (((1,), (1,)), ((), ())),
            preferred_element_type=jnp.float32,
        )

        shifted = []
        for u in range(UNROLL):
            r = start + u - lag
            spot = jnp.maximum(r + edge, 0)
            resid = near_own[0] + far_rolled[spot].astype(jnp.float32)
            resid = resid + (
                sums[slot(r - d), :chans]
                + sums[slot(r), chans : 2 * chans]
                + sums[slot(r + d), 2 * chans :]
            )
            pred = jnp.sum(head * jnp.maximum(resid, 0.0), axis=0, keepdims=True)
            pred_ref[pl.ds(start + u, 1), :] = pred
            offs = offs_first + r - 2 * edge
            inside = jnp.where((offs >= 0) & (offs < offs_count), 1.0, 0.0)
            weight = (
                scored
                * mask_rolled[spot][0:1, :]
                * jnp.where(offs.astype(jnp.float32) < limit, inside, 0.0)
            )
            differ = pred - target_ref[pl.ds(start + u, 1), :]
            own = own_lane & owned(r)
            err = err + jnp.where(own, weight * differ * differ, 0.0)
            dpred = 2.0 * weight * differ / denom
            dres = jnp.where(resid > 0.0, head * dpred, 0.0)
            dres = dres.astype(jnp.bfloat16).astype(jnp.float32)
            own_grad[slot(r)] = jnp.where(own, dres, 0.0).astype(jnp.bfloat16)
            shifted.append(
                jnp.concatenate(
                    [
                        pltpu.roll(dres, width - d, 1).astype(jnp.bfloat16),
                        dres.astype(jnp.bfloat16),
                        pltpu.roll(dres, d, 1).astype(jnp.bfloat16),
                    ],
                    axis=0,
                )
            )
        backed = jnp.dot(
            back_taps, jnp.concatenate(shifted, axis=1), preferred_element_type=jnp.float32
        )

        fresh = []
        for u in range(UNROLL):
            r = start + u
            offs = offs_first + r - 2 * edge
            inside = jnp.where((offs >= 0) & (offs < offs_count), 1.0, 0.0)
            keep = jnp.full((chans, width), inside, jnp.float32).astype(jnp.bfloat16)
            parts = []
            for a in range(3):
                cells = near_shift[a] + far_rolled[r + edge + (a - 1) * d]
                parts.append(jnp.maximum(cells, 0.0) * keep)
            fresh.append(jnp.concatenate(parts, axis=0))
        summed = jnp.dot(
            forward_taps, jnp.concatenate(fresh, axis=1), preferred_element_type=jnp.float32
        )
        for u in range(UNROLL):
            lanes = slice(u * width, (u + 1) * width)
            backs[slot(start + u - lag)] = backed[:, lanes]
            sums[slot(start + u)] = summed[:, lanes]
            stack[slot(start + u)] = fresh[u]
        return err

    err_ref[...] = lax.fori_loop(
        0, total // UNROLL, step, jnp.zeros((1, width), jnp.float32)
    )


def band(pieces, bins, target, head, conv_two, dil, place, denom, rows, tile_rows, extent):
    chans = head.shape[0]
    edge = LARGEST_DILATION
    width = tile_rows + 128
    wide = round_up(tile_rows + rows + 10 * edge, 128)
    total = rows + 6 * edge
    ext = bins.shape[1] + extent + wide + 128
    smem = pl.BlockSpec(memory_space=pltpu.SMEM)
    vmem = pl.BlockSpec(memory_space=pltpu.VMEM)
    return pl.pallas_call(
        functools.partial(band_body, edge, rows),
        out_shape=(
            jax.ShapeDtypeStruct((total, width), jnp.float32),
            jax.ShapeDtypeStruct((1, width), jnp.float32),
            jax.ShapeDtypeStruct((3 * chans, 3 * chans), jnp.float32),
            jax.ShapeDtypeStruct((chans, width), jnp.float32),
            jax.ShapeDtypeStruct((chans, wide), jnp.float32),
        ),
        in_specs=[smem] * 3 + [vmem] * 5,
        out_specs=(vmem,) * 5,
        scratch_shapes=[
            pltpu.VMEM((chans + 8, ext), jnp.float32),
            pltpu.VMEM((chans + 8, ext), jnp.float32),
            pltpu.VMEM((total + 2 * edge, chans, width), jnp.bfloat16),
            pltpu.VMEM((total + 2 * edge, 8, width), jnp.float32),
            pltpu.VMEM((3, chans, width), jnp.bfloat16),
            pltpu.VMEM((2, chans, width), jnp.float32),
            pltpu.VMEM((RING, 3 * chans, width), jnp.bfloat16),
            pltpu.VMEM((RING, 3 * chans, width), jnp.float32),
            pltpu.VMEM((RING, 3 * chans, width), jnp.float32),
            pltpu.VMEM((RING, chans, width), jnp.bfloat16),
            pltpu.VMEM((2, 128, 128), jnp.float32),
        ],
        compiler_params=pltpu.CompilerParams(vmem_limit_bytes=56 * 1024 * 1024),
        cost_estimate=pl.CostEstimate(flops=4000000000, bytes_accessed=2000000, transcendentals=0),
        name="band",
    )(dil, place, denom, pieces, bins, target, head, conv_two)


def shards(
    encoder_in,
    gain_enc,
    conv_one,
    proj_weight,
    conv_two,
    head_weight,
    target,
    valid_bins,
    offset_limit,
    dilations,
):
    chans, encoder_bins = encoder_in.shape
    width_in = conv_one.shape[2]
    second_channels = conv_two.shape[1]
    tile_rows, tile_cols = target.shape
    first_dilation = dilations[0]
    second_dilation = dilations[1]
    activ = jax.nn.gelu(gain_enc[:, None] * encoder_in.astype(jnp.float32)).astype(jnp.bfloat16)
    encs, bins, offs = (lax.axis_size(axis) for axis in ("enc", "bin", "off"))
    group = bins * offs
    rows_piece = 2 * second_channels // group
    framed = gather_framed(activ, encs, bins, offs).reshape(width_in, encoder_bins + 256)
    stacked_enc = jnp.concatenate(
        [
            lax.dynamic_slice_in_dim(framed, 128 + (tap - 1) * first_dilation, encoder_bins, 1)
            for tap in range(3)
        ],
        axis=0,
    )
    weight_one = jnp.transpose(conv_one, (1, 0, 2)).reshape(chans, 3 * width_in)
    conv_out = jnp.dot(weight_one, stacked_enc, preferred_element_type=jnp.float32)
    hidden = (encoder_in.astype(jnp.float32) + conv_out).astype(jnp.bfloat16)
    proj_rows = jnp.transpose(proj_weight, (0, 2, 1)).reshape(2 * second_channels, chans)
    partial_embed = jnp.dot(proj_rows, hidden, preferred_element_type=jnp.float32)
    pieces = exchange(
        partial_embed.reshape(group, 1, rows_piece, encoder_bins), encs, bins, offs, False, 1, "embed"
    )
    framed, hidden_sent, pieces = lax.optimization_barrier((framed, hidden, pieces))
    enc_index = lax.axis_index("enc")
    share = width_in // encs

    def parcel(owner):
        rows = lax.dynamic_slice(framed, (owner * share, 128), (share, encoder_bins))
        return jnp.concatenate([rows, hidden_sent], axis=0)

    whole_side = jnp.zeros((share + chans, encs * encoder_bins), jnp.bfloat16)
    whole_side = lax.dynamic_update_slice(
        whole_side, parcel(enc_index), (0, enc_index * encoder_bins)
    )
    for hop in range(1, encs):
        arrived = lax.ppermute(
            parcel(lax.rem(enc_index + hop, encs)),
            "enc",
            [(i, (i + hop) % encs) for i in range(encs)],
        )
        origin = lax.rem(enc_index + encs - hop, encs)
        whole_side = lax.dynamic_update_slice(whole_side, arrived, (0, origin * encoder_bins))
    sequence_length = encs * encoder_bins
    window_extent = tile_cols * encs * offs
    row_start = lax.axis_index("bin") * tile_rows
    offs_start = (lax.axis_index("enc") * lax.axis_size("off") + lax.axis_index("off")) * tile_cols
    edge = LARGEST_DILATION
    width = tile_rows + 128
    bin_rows = jnp.pad(jnp.stack([valid_bins, offset_limit]), ((0, 6), (0, 0)))
    denom = 1.0 + count_cells(valid_bins, offset_limit)
    framed_target = with_halo(target, (("bin", 0), (("enc", "off"), 1)), edge)
    first_row = 2 * edge + UNROLL
    target_rows = jnp.pad(
        framed_target.T.astype(jnp.float32),
        ((first_row, 2 * edge - UNROLL), (edge, width - tile_rows - 3 * edge)),
    )
    pred_rows, error_lanes, grad_taps, near_lanes, far_lanes = band(
        pieces,
        bin_rows,
        target_rows,
        head_weight.reshape(second_channels, 1),
        conv_two,
        second_dilation.reshape(1),
        jnp.stack([row_start, offs_start, jnp.full((), window_extent, jnp.int32)]).astype(jnp.int32),
        denom.reshape(1),
        tile_cols,
        tile_rows,
        window_extent,
    )
    first_own = first_row + edge
    prediction = pred_rows[
        first_own : first_own + tile_cols, 2 * edge : 2 * edge + tile_rows
    ].T
    near_grad = near_lanes[:, 2 * edge : 2 * edge + tile_rows]
    far_grad = far_lanes[:, 5 * edge : 5 * edge + tile_rows + tile_cols - 1]
    buffer = jnp.zeros((2 * second_channels, sequence_length + window_extent), jnp.float32)
    buffer = lax.dynamic_update_slice(buffer, near_grad, (0, row_start))
    buffer = lax.dynamic_update_slice(buffer, far_grad, (second_channels, row_start + offs_start))
    buffer = buffer[:, :sequence_length].reshape(group, rows_piece, encs, encoder_bins)
    taps_rows, error_rows = grad_taps.shape[0], width // 128
    half = 2 * second_channels
    common = jnp.concatenate(
        [
            jnp.pad(grad_taps, ((0, 0), (0, 128 - taps_rows))),
            error_lanes.reshape(error_rows, 128),
            jnp.zeros((2 * half - taps_rows - error_rows, 128), jnp.float32),
        ]
    )
    common = jnp.transpose(common.reshape(group, 2, rows_piece, 128), (0, 2, 1, 3))
    common = common.reshape(group, 1, rows_piece, 256)
    common = jnp.pad(common, ((0, 0), (0, 0), (0, 0), (0, encoder_bins - 256)))
    outgoing = jnp.concatenate([jnp.transpose(buffer, (0, 2, 1, 3)), common], axis=1)
    summed = exchange(outgoing, encs, bins, offs, True, 2, "grads")
    grad_rows = jnp.transpose(summed[:, :encs], (0, 2, 1, 3)).reshape(half, sequence_length)
    grad_rows = grad_rows.astype(jnp.bfloat16)
    common = summed[:, encs, :, :256].reshape(group, rows_piece, 2, 128)
    common = jnp.transpose(common, (0, 2, 1, 3)).reshape(2 * half, 128)
    grad_conv_two = jnp.transpose(
        common[:taps_rows, :taps_rows].reshape(3, second_channels, 3, second_channels), (0, 2, 1, 3)
    ).reshape(9, second_channels, second_channels)
    total_error = jnp.sum(common[taps_rows : taps_rows + error_rows])
    dhidden = jnp.dot(proj_rows.T, grad_rows, preferred_element_type=jnp.float32).astype(
        jnp.bfloat16
    )
    activ_side = jnp.pad(whole_side[:share], ((0, 0), (edge, edge)))
    hidden_side = whole_side[share:]
    across = (((1,), (1,)), ((), ()))
    grad_proj = lax.dot_general(
        hidden_side, grad_rows, across, preferred_element_type=jnp.float32
    )
    grad_proj = jnp.stack([grad_proj[:, :second_channels], grad_proj[:, second_channels:]])
    grad_conv_one = jnp.stack(
        [
            lax.dot_general(
                dhidden,
                lax.dynamic_slice_in_dim(
                    activ_side, edge + (tap - 1) * first_dilation, sequence_length, 1
                ),
                across,
                preferred_element_type=jnp.float32,
            )
            for tap in range(3)
        ]
    )
    loss_mean = (total_error / denom).reshape(1)
    return (prediction, loss_mean, grad_conv_two, grad_proj, grad_conv_one)


def solution(mesh):
    in_specs = (
        P(("bin", "off"), "enc"),
        P(("bin", "off")),
        P(None, ("bin", "off"), None),
        P(None, ("bin", "off"), None),
        P(),
        P(),
        P("bin", ("enc", "off")),
        P(),
        P(),
        P(),
    )
    out_specs = (
        P("bin", ("enc", "off")),
        P(),
        P(),
        P(None, ("bin", "off"), None),
        P(None, ("bin", "off"), "enc"),
    )
    return jax.shard_map(shards, mesh=mesh, in_specs=in_specs, out_specs=out_specs, check_vma=False)
```
